512 devices in a mesh: req: 128 (over y, z, core), head: 4 (over x).
Axes of the slice: x: 4, y: 8, z: 8, core: 2. Of those that a mesh axis runs over, the one named last changes fastest.
Arguments:
- queries: bfloat16 [8192, 4, 8192], P('req', None, 'head'), may hold values from -600 to 600
- new_kv: bfloat16 [8192, 4, 2, 1024], P('req', None, None, 'head'), may hold values from -6 to 6
- suffix_kv: bfloat16 [8192, 2, 32, 1024], P('req', None, None, 'head'), may hold values from -6 to 6
- prefix_kv: bfloat16 [128, 2, 512, 1024], P('req', None, None, 'head'), may hold values from -6 to 6
- prefix_id: int32 [8192, 1], P(('req', 'head')), may hold values from 0 to 127; in each aligned block of 64 rows (0 to 63, 64 to 127, ...) at most 2 rows name the same one
- suffix_len: int32 [8192], P(('req', 'head')), may hold values from 1 to 32, 131072 in all
- owner_map: int32 [128], replicated, may hold values from 0 to 127, each once
Outputs:
- attended: bfloat16 [8192, 4, 8192], P('req', None, 'head')
The draws below stay inside these ranges and needn't reach their ends.
Inputs may be any that keep to these rules, and one draw needn't show every extreme that they name: `prefix_id`: at most 2 of the requests of one index of req name the same prefix, and in every draw some prefix is named by exactly 2 of them; popularity of prefixes is skewed. `owner_map`: each storage slot holds exactly one prefix.
All inputs are finite; a program needn't handle non-finite values. No bound on the sum of `suffix_len` on one device may be relied on, other than what follows from the above.
Results may differ from the reference program's by a relative error of at most 0.0051.
Values may be sent and summed in bfloat16 or wider, within the bound.
No kernel may reach another device: no remote copies, remote signals or barrier semaphores. Data moves between devices by JAX's collectives and lax.ppermute only.
A program may use at most 128 MiB of HBM per device.

```python
import math
import jax
import jax.numpy as jnp
import numpy as np
from jax import lax

H = 64
KVH = 8
HD = 128
ROW_DEV = 64
PLEN = 512
SUF = 32
STEPS = 4
CAP = 2
NPREF = 128
ROWS = 8192


def draw_queries(key, part):
    key = jax.random.fold_in(key, 11)
    base = jax.random.normal(key, (ROWS, STEPS, H * HD), jnp.float32) * 2.5
    base = jnp.clip(base, -15.0, 15.0)
    return base.astype(jnp.bfloat16)


def level_of(key, shape, pieces, low, top_value):
    def one(axis_at, shards_of):
        steps = jax.random.uniform(jax.random.fold_in(jax.random.fold_in(key, 6), axis_at), (shards_of,), jnp.float32, low / len(pieces), top_value / len(pieces))
        return jnp.repeat(jnp.exp(steps), shape[axis_at] // shards_of).reshape((-1,) + (1,) * (len(shape) - axis_at - 1))

    gain = one(*pieces[0])
    for cut in pieces[1:]:
        gain = gain * one(*cut)
    return gain


def length_profile(count, total, limit, slope):
    loads = [(1 << 20) // math.isqrt(grade ** slope) + 1 for grade in range(2, count + 1)]
    spare, given = total - limit - (count - 1), [1] * (count - 1)
    while spare > 0:
        candidates = [i for i in range(count - 1) if given[i] < limit]
        whole, budget = sum([loads[i] for i in candidates]), spare
        for i in candidates:
            extra = min(limit - given[i], max(1, budget * loads[i] // whole), spare)
            given[i] = given[i] + extra
            spare = spare - extra
    return np.array([limit] + given)


def ragged_sizes(rng, number_of, total, limit, skew):
    if number_of == 2:
        one = jax.random.randint(rng, (), max(1, total - limit), min(limit, total - 1) + 1)
        return jnp.stack([one, total - one])
    lengths = jnp.asarray(length_profile(number_of, total, limit, skew), jnp.int32)
    twos = (number_of - 1) // 2
    giver, receiver = lengths[1:1 + 2 * twos:2], lengths[2:2 + 2 * twos:2]
    room = jnp.minimum(giver - 1, limit - receiver)
    passed = jax.random.randint(jax.random.fold_in(rng, 1), (twos,), 0, 1 << 20) % (room + 1)
    lengths = lengths.at[1:1 + 2 * twos:2].set(giver - passed).at[2:2 + 2 * twos:2].set(receiver + passed)
    return lengths[jax.random.permutation(jax.random.fold_in(rng, 2), number_of)]


def shared_out(stream_key, own, number, rows, amount, top, reach, slope):
    ranking = jax.random.permutation(stream_key, amount)
    crowded, common = shares(amount, rows * top, reach, slope, True), shares(amount, rows * top, reach, slope, False)
    places = jnp.arange(amount)

    def named(lengths, rotation):
        used = int((lengths > 0).sum())
        fixed = max(1, used // 4)
        passed = fixed + (places - fixed + rotation * (used - fixed)) % max(1, amount - fixed)
        return jnp.zeros((amount,), jnp.int32).at[ranking[jnp.where(places < fixed, places, passed)]].set(jnp.asarray(lengths, jnp.int32))

    lengths = jnp.where(number % 4 == 0, named(crowded, number // 4), named(common, number - number // 4 - 1))
    mixed = jax.random.permutation(jax.random.fold_in(own, 3), amount)
    giver, receiver = mixed[0:amount // 2 * 2:2], mixed[1:amount // 2 * 2:2]
    room = jnp.minimum(lengths[giver] - 1, reach - lengths[receiver]) // 2
    room = jnp.where((giver == ranking[0]) | (receiver == ranking[0]) | (lengths[receiver] == 0), 0, jnp.maximum(room, 0))
    passed = jax.random.randint(jax.random.fold_in(own, 4), (amount // 2,), 0, 1 << 20) % (room + 1)
    lengths = lengths.at[giver].add(-passed).at[receiver].add(passed)
    items = jnp.searchsorted(jnp.cumsum(lengths), jnp.arange(rows * top), side="right").astype(jnp.int32)
    grid = items.reshape(top, rows).T
    grid = grid[jax.random.permutation(jax.random.fold_in(own, 1), rows)]
    rotation = jax.random.randint(jax.random.fold_in(own, 2), (rows, 1), 0, top)
    return jnp.take_along_axis(grid, (jnp.arange(top)[None, :] + rotation) % top, axis=1)


def shares(number_of, total, limit, slope, full):
    weights = [(1 << 20) // math.isqrt(grade ** slope) + 1 for grade in range(1, number_of + 1)]
    largest = limit if full else min(limit, max(-(-total // number_of), total * weights[0] // sum(weights)))
    least = 1 if total - largest >= number_of - 1 else 0
    holding, spare = [largest] + [least] * (number_of - 1), total - largest - least * (number_of - 1)
    while spare > 0:
        free = [i for i in range(1, number_of) if holding[i] < largest] or [i for i in range(1, number_of) if holding[i] < limit]
        whole, left = sum([weights[i] for i in free]), spare
        for i in free:
            extra = min(limit - holding[i], max(1, left * weights[i] // whole), spare)
            holding[i] = holding[i] + extra
            spare = spare - extra
    return np.array(holding)


def scatter_about(stream_key, shape, spread, limit, cuts=(), held_as=jnp.bfloat16):
    array = spread * jax.random.normal(stream_key, shape, jnp.float32)
    if cuts:
        array = array * level_of(stream_key, shape, cuts, -0.22, 0.18)
    return jnp.clip(array, -limit, limit).astype(held_as)


def setup_inputs(seed: int = 0) -> dict:
    arg_keys = jax.random.split(jax.random.key(seed), 8)
    queries = draw_queries(jax.random.fold_in(arg_keys[7], 71), 0)
    new_kv = scatter_about(arg_keys[1], (ROWS, STEPS, 2, KVH * HD), 1.0, 6.0, ((0, 128), (3, 4)))
    suffix_kv = scatter_about(arg_keys[2], (ROWS, 2, SUF, KVH * HD), 1.0, 6.0, ((0, 128), (3, 4)))
    prefix_kv = scatter_about(arg_keys[3], (NPREF, 2, PLEN, KVH * HD), 1.0, 6.0, ((0, 128), (3, 4)))
    prefix_id_keys = jax.random.split(jax.random.fold_in(arg_keys[4], 1), ROWS // ROW_DEV)
    prefix_id_turns = jax.random.permutation(jax.random.fold_in(arg_keys[4], 3), ROWS // ROW_DEV)
    prefix_id = jax.vmap(lambda own, number: shared_out(jax.random.fold_in(arg_keys[4], 2), own, number, ROW_DEV, NPREF, 1, CAP, 2))(prefix_id_keys, prefix_id_turns).reshape((ROWS, 1))
    suffix_len = ragged_sizes(arg_keys[5], ROWS, ROWS * SUF // 2, SUF, 2).astype(jnp.int32)
    owner_map = jax.random.permutation(arg_keys[6], NPREF).astype(jnp.int32)
    return dict(queries=queries, new_kv=new_kv, suffix_kv=suffix_kv, prefix_kv=prefix_kv, prefix_id=prefix_id, suffix_len=suffix_len, owner_map=owner_map)


def rounded(values):
    return lax.optimization_barrier(values.astype(jnp.bfloat16)).astype(jnp.float32)


def reference(queries, new_kv, suffix_kv, prefix_kv, prefix_id, suffix_len, owner_map):
    group = H // KVH
    scale = 1.0 / (HD ** 0.5)
    slots = owner_map[prefix_id[:, 0]]
    block = 8
    count = ROWS // block
    span = SUF + STEPS

    def one_block(items):
        query, fresh, cache, slot, length = items
        stored = prefix_kv[slot]
        qf = query.astype(jnp.float32).reshape(block, STEPS, KVH, group, HD)
        keys_p = stored[:, 0].astype(jnp.float32).reshape(block, PLEN, KVH, HD)
        vals_p = stored[:, 1].astype(jnp.float32).reshape(block, PLEN, KVH, HD)
        score_p = jnp.einsum('rtkgd,rpkd->rtkgp', qf, keys_p) * scale
        max_p = jnp.max(score_p, axis=-1)
        weight_p = jnp.exp(score_p - max_p[..., None])
        total_p = jnp.sum(weight_p, axis=-1)
        out_p = jnp.einsum('rtkgp,rpkd->rtkgd', rounded(weight_p), vals_p) / total_p[..., None]
        out_p = rounded(out_p)
        keys_s = jnp.concatenate([cache[:, 0], fresh[:, :, 0]], axis=1).astype(jnp.float32).reshape(block, span, KVH, HD)
        vals_s = jnp.concatenate([cache[:, 1], fresh[:, :, 1]], axis=1).astype(jnp.float32).reshape(block, span, KVH, HD)
        position = jnp.arange(span, dtype=jnp.int32)
        stepidx = jnp.arange(STEPS, dtype=jnp.int32)
        live = jnp.where(position[None, None, :] < SUF,
                         position[None, None, :] < length[:, None, None],
                         (position[None, None, :] - SUF) <= stepidx[None, :, None])
        score_s = jnp.einsum('rtkgd,rpkd->rtkgp', qf, keys_s) * scale
        score_s = jnp.where(live[:, :, None, None, :], score_s, -jnp.inf)
        max_s = jnp.max(score_s, axis=-1)
        weight_s = jnp.where(live[:, :, None, None, :], jnp.exp(score_s - max_s[..., None]), 0.0)
        total_s = jnp.sum(weight_s, axis=-1)
        out_s = jnp.einsum('rtkgp,rpkd->rtkgd', rounded(weight_s), vals_s) / total_s[..., None]
        top = jnp.maximum(max_p, max_s)
        share_p = total_p * jnp.exp(max_p - top)
        share_s = total_s * jnp.exp(max_s - top)
        mixed = (share_p[..., None] * out_p + share_s[..., None] * out_s) / (share_p + share_s)[..., None]
        return mixed.reshape(block, STEPS, H * HD).astype(jnp.bfloat16)

    result = lax.map(one_block, (queries.reshape(count, block, STEPS, H * HD),
                                 new_kv.reshape(count, block, STEPS, 2, KVH * HD),
                                 suffix_kv.reshape(count, block, 2, SUF, KVH * HD),
                                 slots.reshape(count, block),
                                 suffix_len.reshape(count, block)))
    return result.reshape(ROWS, STEPS, H * HD)
```

```python
import jax
import jax.numpy as jnp
from jax import lax
from jax.experimental import pallas as pl
from jax.experimental.pallas import tpu as pltpu
from jax.sharding import PartitionSpec as P

HD = 128
STEPS = 4
SIDE = 8
CORES = 2
GROUP = 8
QROWS = STEPS * GROUP
BATCH = 4
LOG2E = 1.4426950408889634
NT = (((1,), (1,)), ((), ()))


def device(y, z, c):
    return (y * SIDE + z) * CORES + c


ALONG_Y = [[[device(y, z, c) for y in range(SIDE)] for z in range(SIDE)] for c in range(CORES)]
ALONG_Z = [[[device(y, z, c) for z in range(SIDE)] for y in range(SIDE)] for c in range(CORES)]
ROW_GROUPS = ALONG_Y[0] + ALONG_Z[1]
EMPTY = 255


PREFIX_GROUPS = ALONG_Z[0] + ALONG_Y[1]
SWAP = [(i, i ^ 1) for i in range(SIDE * SIDE * CORES)]


def softmax_parts(score, scale):
    largest = jnp.max(score, axis=-1, keepdims=True)
    weight = jnp.exp2((score - largest) * (scale * LOG2E))
    total = jnp.sum(weight, axis=-1, keepdims=True)
    return weight, total, largest * scale


def send_kernel(source_ref, place_ref, query_ref, out_ref):
    chips, tiles = out_ref.shape[:2]
    slots = tiles - 1

    def one_chip(chip, carry):
        for i in range(slots):
            out_ref[chip, i] = query_ref[source_ref[chip * slots + i]]
        places = jnp.broadcast_to(place_ref[chip], (QROWS, HD))
        out_ref[chip, slots] = places.astype(jnp.bfloat16)
        return carry

    lax.fori_loop(0, chips, one_chip, 0)


def send(source, places, query):
    chips = places.shape[0]
    slots = source.shape[0] // chips
    return pl.pallas_call(
        send_kernel,
        out_shape=jax.ShapeDtypeStruct((chips, slots + 1) + query.shape[1:], query.dtype),
        in_specs=[pl.BlockSpec(memory_space=pltpu.SMEM)]
        + [pl.BlockSpec(memory_space=pltpu.VMEM)] * 2,
        out_specs=pl.BlockSpec(memory_space=pltpu.VMEM),
        compiler_params=pltpu.CompilerParams(vmem_limit_bytes=12 << 20),
        name="send",
    )(source, places, query)


def visit_kernel(
    note_ref, query_ref, far_ref, out_ref, kv_ref, stat, codes, places, lists, counts, batches, sems
):
    prefixes = pltpu.make_async_copy(far_ref, kv_ref, sems.at[1])
    prefixes.start()
    sources, slots = query_ref.shape[0], query_ref.shape[1] - 1
    held = kv_ref.shape[0]
    length = kv_ref.shape[1] // 2
    room = lists.shape[0] // held
    scale = 1.0 / HD**0.5
    for source in range(sources):
        row = query_ref[source, slots, :1].astype(jnp.float32)
        codes[source : source + 1] = row.astype(jnp.int32)
    to_scalars = pltpu.make_async_copy(codes, places, sems.at[0])
    to_scalars.start()
    stat[...] = jnp.zeros_like(stat)
    lane = lax.broadcasted_iota(jnp.int32, (QROWS, HD), 1)
    piece = lane // 32
    within = lane % 32
    for i in range(held):
        counts[i] = 0
    to_scalars.wait()

    def sort_source(source, filled):
        for slot in range(slots):
            place = places[source, slot]
            valid = place < held
            place = jnp.where(valid, place, 0)
            turn = counts[place]
            opens = valid & (turn % BATCH == 0)

            @pl.when(valid)
            def _(place=place, turn=turn, slot=slot):
                lists[place * room + turn] = source * slots + slot
                counts[place] = turn + 1

            @pl.when(opens)
            def _(place=place, turn=turn, filled=filled):
                batches[filled] = place * room + turn

            filled = filled + opens.astype(jnp.int32)
        return filled

    count = lax.fori_loop(0, sources, sort_source, 0)
    prefixes.wait()
    note = jnp.broadcast_to(note_ref[:1], (QROWS, HD)).astype(jnp.bfloat16)
    for source in range(sources):
        out_ref[source, slots + 1] = note

    def one_pair(pair, carry):
        work = []
        for half in range(2):
            start = batches[jnp.minimum(2 * pair + half, count - 1)]
            place = start // room
            last = place * room + counts[place] - 1
            code = [lists[jnp.minimum(start + i, last)] for i in range(BATCH)]
            work.append((place, [(c // slots, c % slots) for c in code]))
        scores = []
        for place, code in work:
            query = jnp.concatenate([query_ref[source, slot] for source, slot in code], axis=0)
            scores.append(
                lax.dot_general(
                    query, kv_ref[place, :length], NT, preferred_element_type=jnp.float32
                )
            )
        parts = [softmax_parts(score, scale) for score in scores]
        for (place, code), (weight, total, top) in zip(work, parts):
            mixed = jnp.dot(
                weight.astype(jnp.bfloat16),
                kv_ref[place, length : 2 * length],
                preferred_element_type=jnp.float32,
            )
            mixed = (mixed / total).astype(jnp.bfloat16)
            hi = top.astype(jnp.bfloat16).astype(jnp.float32)
            rest = top - hi
            mid = rest.astype(jnp.bfloat16).astype(jnp.float32)
            rest = (rest - mid) + jnp.log(total)
            low = rest.astype(jnp.bfloat16).astype(jnp.float32)
            last = rest - low
            for i, (source, slot) in enumerate(code):
                part = slice(i * QROWS, (i + 1) * QROWS)
                out_ref[source, slot] = mixed[part]
                value = jnp.where(
                    piece < 2,
                    jnp.where(piece == 0, hi[part], mid[part]),
                    jnp.where(piece == 2, low[part], last[part]),
                )
                stat[source] = jnp.where(within == slot, value, stat[source])
        return carry

    lax.fori_loop(0, (count + 1) // 2, one_pair, 0)
    out_ref[:, slots] = stat[...].astype(jnp.bfloat16)


def visit(note, query, kv):
    sources, tiles = query.shape[:2]
    held = kv.shape[0]
    room = 2 * CORES * SIDE
    return pl.pallas_call(
        visit_kernel,
        out_shape=jax.ShapeDtypeStruct((sources, tiles + 1) + query.shape[2:], query.dtype),
        in_specs=[pl.BlockSpec(memory_space=pltpu.VMEM)] * 2
        + [pl.BlockSpec(memory_space=pl.ANY)],
        out_specs=pl.BlockSpec(memory_space=pltpu.VMEM),
        scratch_shapes=[
            pltpu.VMEM(kv.shape, kv.dtype),
            pltpu.VMEM((sources, QROWS, HD), jnp.float32),
            pltpu.VMEM((sources, HD), jnp.int32),
            pltpu.SMEM((sources, HD), jnp.int32),
            pltpu.SMEM((held * room,), jnp.int32),
            pltpu.SMEM((held,), jnp.int32),
            pltpu.SMEM((held * room // BATCH,), jnp.int32),
            pltpu.SemaphoreType.DMA((2,)),
        ],
        compiler_params=pltpu.CompilerParams(vmem_limit_bytes=24 << 20),
        name="visit",
    )(note, query, kv)


def suffix_kernel(length_ref, query_ref, key_ref, value_ref, out_ref, top_ref, total_ref):
    kv_heads, rows = query_ref.shape[:2]
    span = key_ref.shape[1]
    cache = span - 16
    scale = 1.0 / HD**0.5
    base = pl.program_id(0) * rows
    slot = lax.broadcasted_iota(jnp.int32, (QROWS, span), 1)
    step = lax.broadcasted_iota(jnp.int32, (QROWS, span), 0) // GROUP
    fresh = (slot >= cache) & (slot - cache <= step)
    cols = [slice(k * HD, (k + 1) * HD) for k in range(kv_heads)]
    items = [(k, r) for r in range(rows) for k in range(kv_heads)]
    scores = []
    for k, r in items:
        score = lax.dot_general(
            query_ref[k, r], key_ref[r, :, cols[k]], NT, preferred_element_type=jnp.float32
        )
        live = fresh | (slot < jnp.minimum(length_ref[base + r], cache))
        scores.append(jnp.where(live, score, -jnp.inf))
    weight, total, top = softmax_parts(jnp.concatenate(scores, axis=0), scale)
    weight = weight.astype(jnp.bfloat16)
    mixed = [
        jnp.dot(
            weight[i * QROWS : (i + 1) * QROWS],
            value_ref[r, :, cols[k]],
            preferred_element_type=jnp.float32,
        )
        for i, (k, r) in enumerate(items)
    ]
    top = jnp.broadcast_to(top, (len(items) * QROWS, HD))
    total = jnp.broadcast_to(total, (len(items) * QROWS, HD))
    for i, (k, r) in enumerate(items):
        part = slice(i * QROWS, (i + 1) * QROWS)
        out_ref[k, r] = mixed[i]
        top_ref[k, r] = top[part]
        total_ref[k, r] = total[part]


def suffix(lengths, query, keys, values):
    kv_heads, rows = query.shape[:2]
    chunk = 8
    span = keys.shape[1]
    by_row = pl.BlockSpec((kv_heads, chunk, QROWS, HD), lambda i, n: (0, i, 0, 0))
    by_slot = pl.BlockSpec((chunk, span, kv_heads * HD), lambda i, n: (i, 0, 0))
    return pl.pallas_call(
        suffix_kernel,
        out_shape=(jax.ShapeDtypeStruct((kv_heads, rows, QROWS, HD), jnp.float32),) * 3,
        grid_spec=pltpu.PrefetchScalarGridSpec(
            num_scalar_prefetch=1,
            grid=(rows // chunk,),
            in_specs=[by_row, by_slot, by_slot],
            out_specs=(by_row,) * 3,
        ),
        compiler_params=pltpu.CompilerParams(vmem_limit_bytes=16 << 20),
        cost_estimate=pl.CostEstimate(
            flops=4 * rows * kv_heads * QROWS * span * HD,
            bytes_accessed=8 << 20,
            transcendentals=rows * kv_heads * QROWS * span,
        ),
        name="suffix",
    )(lengths, query, keys, values)


def join_kernel(
    core_ref, table_ref, mine_ref, theirs_ref, suf_ref, top_ref, total_ref, out_ref
):
    rows = suf_ref.shape[1]
    for which, block in enumerate((mine_ref, theirs_ref)):
        head = which ^ core_ref[0]

        def one_row(r, carry, block=block, which=which, head=head):
            far = block[table_ref[(3 * which + 1) * rows + r]].astype(jnp.float32)
            far = far + pltpu.roll(far, HD - 32, 1)
            lane = table_ref[(3 * which + 2) * rows + r]
            max_p = jnp.take_along_axis(far, jnp.full(far.shape, lane, jnp.int32), axis=1)
            log_p = jnp.take_along_axis(far, jnp.full(far.shape, lane + 64, jnp.int32), axis=1)
            max_s = top_ref[head, r]
            top = jnp.maximum(max_p, max_s)
            share_p = jnp.exp((max_p - top) + log_p)
            scale_s = jnp.exp(max_s - top)
            value = block[table_ref[3 * which * rows + r]].astype(jnp.float32)
            mixed = share_p * value + scale_s * suf_ref[head, r]
            whole = share_p + scale_s * total_ref[head, r]
            out_ref[head, r] = (mixed / whole).astype(jnp.bfloat16)
            return carry

        lax.fori_loop(0, rows, one_row, 0, unroll=8)


def join(core, table, mine, theirs, near):
    kv_heads, rows = near[0].shape[:2]
    return pl.pallas_call(
        join_kernel,
        out_shape=jax.ShapeDtypeStruct((kv_heads, rows, QROWS, HD), jnp.bfloat16),
        in_specs=[pl.BlockSpec(memory_space=pltpu.SMEM)] * 2
        + [pl.BlockSpec(memory_space=pltpu.VMEM)] * 5,
        out_specs=pl.BlockSpec(memory_space=pltpu.VMEM),
        compiler_params=pltpu.CompilerParams(vmem_limit_bytes=24 << 20),
        name="join",
    )(core, table, mine, theirs, *near)


def shards(queries, new_kv, suffix_kv, prefix_kv, prefix_id, suffix_len, owner_map):
    rows, _, width = queries.shape
    kv_heads = new_kv.shape[-1] // HD
    me = lax.axis_index("req")
    core = me % CORES

    def swap(array):
        return lax.ppermute(array, "req", SWAP)

    stored = prefix_kv[0].reshape(-1, kv_heads, HD)
    mine, other = stored[:, 0], stored[:, 1]
    mine, other = jnp.where(core == 0, mine, other), jnp.where(core == 0, other, mine)
    mine, other, prefix_id = lax.optimization_barrier((mine, other, prefix_id))
    kv = lax.all_gather(
        jnp.stack([mine, swap(other)]),
        "req",
        axis_index_groups=PREFIX_GROUPS,
        axis=0,
        tiled=True,
    )

    heads = lax.axis_size("head")
    chip_size = heads * CORES
    chips = [[c * chip_size + i for i in range(chip_size)] for c in range(SIDE * SIDE)]
    meta = jnp.stack([prefix_id[:, 0], suffix_len])
    position = core * heads + lax.axis_index("head")
    spot = jnp.arange(chip_size, dtype=jnp.int32)[:, None, None] == position
    meta = lax.psum(jnp.where(spot, meta, 0), ("req", "head"), axis_index_groups=chips)
    ids = meta[:, 0].reshape(CORES, rows)
    lengths = lax.dynamic_index_in_dim(meta[:, 1].reshape(CORES, rows), core, 0, keepdims=False)
    ids = jnp.where(core == 0, ids, ids[::-1])
    table = owner_map.shape[0]
    picked = ids[..., None] == jnp.arange(table, dtype=jnp.int32)
    slot = jnp.sum(jnp.where(picked, owner_map, 0), axis=-1)

    def coordinate(slot, along_y):
        return jnp.where(along_y, slot // (CORES * SIDE), (slot // CORES) % SIDE)

    row = jnp.arange(rows, dtype=jnp.int32)
    before = row[None, :] < row[:, None]

    def rank_of(goal):
        same = goal[..., None, :] == goal[..., :, None]
        return jnp.sum(jnp.where(same & before, 1, 0), axis=-1)

    capacity = rows // 4
    rounds = 2
    slots = CORES * capacity
    wide, narrow = slots + 2, capacity + 1
    goal, cross_goal = coordinate(slot, core == 0), coordinate(slot, core != 0)
    rank, cross_rank = rank_of(goal), rank_of(cross_goal)
    fullest = 1 + jnp.maximum(jnp.max(rank), jnp.max(cross_rank))
    place = cross_goal * CORES + jnp.where(slot % CORES == core, 0, 1)

    query = queries.reshape(rows, STEPS, kv_heads, GROUP, HD)
    query = jnp.transpose(query, (2, 0, 1, 3, 4)).reshape(kv_heads, rows, QROWS, HD)
    own_rows = lax.dynamic_index_in_dim(query, core, 0, keepdims=False)
    other_rows = swap(lax.dynamic_index_in_dim(query, 1 - core, 0, keepdims=False))
    both = jnp.concatenate([own_rows, other_rows])

    def pack(turn):
        chip = jnp.arange(SIDE, dtype=jnp.int32)[:, None, None, None]
        spot = turn * capacity + jnp.arange(capacity, dtype=jnp.int32)[:, None]
        sent = (goal[:, None, :] == chip) & (rank[:, None, :] == spot)
        index = jnp.arange(CORES * rows, dtype=jnp.int32).reshape(CORES, 1, rows)
        from_row = jnp.sum(jnp.where(sent, index, 0), axis=-1).reshape(-1)
        places = EMPTY + jnp.sum(jnp.where(sent, place[:, None, :] - EMPTY, 0), axis=-1)
        places = places.astype(jnp.float32).reshape(SIDE, 1, slots)
        places = jnp.pad(places, ((0, 0), (0, 0), (0, HD - slots)), constant_values=EMPTY)
        at_end = jnp.arange(HD, dtype=jnp.int32) == HD - 1
        places = jnp.where(at_end, fullest.astype(jnp.float32), places)
        return send(from_row, places, both)

    def trade(blocks):
        return lax.all_to_all(blocks, "req", 0, 0, axis_index_groups=ROW_GROUPS, tiled=True)

    outgoing = pack(0)
    outgoing, lengths = lax.optimization_barrier((outgoing, lengths))
    arrived = trade(outgoing)
    pad = jnp.zeros((rows, 16 - STEPS, kv_heads * HD), jnp.bfloat16)
    keys = jnp.concatenate([suffix_kv[:, 0], new_kv[:, :, 0], pad], axis=1)
    values = jnp.concatenate([suffix_kv[:, 1], new_kv[:, :, 1], pad], axis=1)
    near = suffix(lengths, query, keys, values)
    arrived, near = lax.optimization_barrier((arrived, near))
    note = jnp.max(arrived[:, slots, 0, HD - 1].astype(jnp.float32))
    note = jnp.broadcast_to(note, (8, HD))
    note = jnp.maximum(note, swap(note))

    def come_home(done):
        back = trade(done)
        theirs = swap(back[:, capacity : slots + 1])
        fullest = jnp.max(back[:, slots + 1, 0].astype(jnp.float32))
        return back.reshape(-1, QROWS, HD), theirs.reshape(-1, QROWS, HD), fullest

    cross_goal, cross_rank = cross_goal[0], cross_rank[0]
    turn, cross_turn = rank[0] // capacity, cross_rank // capacity
    at, cross_at = rank[0] % capacity, cross_rank % capacity
    base = (turn * SIDE + goal[0]) * wide
    cross_base = (cross_turn * SIDE + cross_goal) * narrow
    home = jnp.stack(
        [
            base + at,
            base + slots,
            at,
            cross_base + cross_at,
            cross_base + capacity,
            capacity + cross_at,
        ]
    ).reshape(-1)
    which = core.reshape(1).astype(jnp.int32)
    arrived, home = lax.optimization_barrier((arrived, home))
    back, theirs, fullest = come_home(visit(note, arrived, kv))

    def finish(back, theirs, both, note, kv, near):
        return join(which, home, back, theirs, near)

    def finish_rest(back, theirs, both, note, kv, near):
        backs, others = [back], [theirs]
        for turn in range(1, rounds):
            done = visit(note, trade(pack(turn)), kv)
            more = come_home(done)
            backs.append(more[0])
            others.append(more[1])
        return join(which, home, jnp.concatenate(backs), jnp.concatenate(others), near)

    out = lax.cond(fullest <= capacity, finish, finish_rest, back, theirs, both, note, kv, near)
    out = out.reshape(kv_heads, rows, STEPS, GROUP, HD)
    return jnp.transpose(out, (1, 2, 0, 3, 4)).reshape(rows, STEPS, width)


def solution(mesh):
    return jax.shard_map(
        shards,
        mesh=mesh,
        in_specs=(
            P("req", None, "head"),
            P("req", None, None, "head"),
            P("req", None, None, "head"),
            P("req", None, None, "head"),
            P(("req", "head"), None),
            P(("req", "head")),
            P(),
        ),
        out_specs=P("req", None, "head"),
        check_vma=False,
    )
```

```python
import jax
import jax.numpy as jnp
from jax import lax
from jax.experimental import pallas as pl
from jax.experimental.pallas import tpu as pltpu
from jax.sharding import PartitionSpec as P

HD = 128
STEPS = 4
SIDE = 8
CORES = 2
GROUP = 8
QROWS = STEPS * GROUP
BATCH = 4
LOG2E = 1.4426950408889634
NT = (((1,), (1,)), ((), ()))


def device(y, z, c):
    return (y * SIDE + z) * CORES + c


ALONG_Y = [[[device(y, z, c) for y in range(SIDE)] for z in range(SIDE)] for c in range(CORES)]
ALONG_Z = [[[device(y, z, c) for z in range(SIDE)] for y in range(SIDE)] for c in range(CORES)]
ROW_GROUPS = ALONG_Y[0] + ALONG_Z[1]
EMPTY = 255


PREFIX_GROUPS = ALONG_Z[0] + ALONG_Y[1]
SWAP = [(i, i ^ 1) for i in range(SIDE * SIDE * CORES)]


def softmax_parts(score, scale):
    largest = jnp.max(score, axis=-1, keepdims=True)
    weight = jnp.exp2((score - largest) * (scale * LOG2E))
    total = jnp.sum(weight, axis=-1, keepdims=True)
    return weight, total, largest * scale


def send_kernel(source_ref, place_ref, query_ref, out_ref):
    chips, tiles = out_ref.shape[:2]
    slots = tiles - 1

    def one_chip(chip, carry):
        for i in range(slots):
            out_ref[chip, i] = query_ref[source_ref[chip * slots + i]]
        places = jnp.broadcast_to(place_ref[chip], (QROWS, HD))
        out_ref[chip, slots] = places.astype(jnp.bfloat16)
        return carry

    lax.fori_loop(0, chips, one_chip, 0)


def send(source, places, query):
    chips = places.shape[0]
    slots = source.shape[0] // chips
    return pl.pallas_call(
        send_kernel,
        out_shape=jax.ShapeDtypeStruct((chips, slots + 1) + query.shape[1:], query.dtype),
        in_specs=[pl.BlockSpec(memory_space=pltpu.SMEM)]
        + [pl.BlockSpec(memory_space=pltpu.VMEM)] * 2,
        out_specs=pl.BlockSpec(memory_space=pltpu.VMEM),
        compiler_params=pltpu.CompilerParams(vmem_limit_bytes=12 << 20),
        name="send",
    )(source, places, query)


def visit_kernel(
    note_ref, query_ref, far_ref, out_ref, kv_ref, stat, codes, places, lists, counts, batches, sems
):
    prefixes = pltpu.make_async_copy(far_ref, kv_ref, sems.at[1])
    prefixes.start()
    sources, slots = query_ref.shape[0], query_ref.shape[1] - 1
    held = kv_ref.shape[0]
    length = kv_ref.shape[1] // 2
    room = lists.shape[0] // held
    scale = 1.0 / HD**0.5
    for source in range(sources):
        row = query_ref[source, slots, :1].astype(jnp.float32)
        codes[source : source + 1] = row.astype(jnp.int32)
    to_scalars = pltpu.make_async_copy(codes, places, sems.at[0])
    to_scalars.start()
    stat[...] = jnp.zeros_like(stat)
    lane = lax.broadcasted_iota(jnp.int32, (QROWS, HD), 1)
    piece = lane // 32
    within = lane % 32
    for i in range(held):
        counts[i] = 0
    to_scalars.wait()

    def sort_source(source, filled):
        for slot in range(slots):
            place = places[source, slot]
            valid = place < held
            place = jnp.where(valid, place, 0)
            turn = counts[place]
            opens = valid & (turn % BATCH == 0)

            @pl.when(valid)
            def _(place=place, turn=turn, slot=slot):
                lists[place * room + turn] = source * slots + slot
                counts[place] = turn + 1

            @pl.when(opens)
            def _(place=place, turn=turn, filled=filled):
                batches[filled] = place * room + turn

            filled = filled + opens.astype(jnp.int32)
        return filled

    count = lax.fori_loop(0, sources, sort_source, 0)
    prefixes.wait()
    note = jnp.broadcast_to(note_ref[:1], (QROWS, HD)).astype(jnp.bfloat16)
    for source in range(sources):
        out_ref[source, slots + 1] = note

    def one_pair(pair, carry):
        work = []
        for half in range(2):
            start = batches[jnp.minimum(2 * pair + half, count - 1)]
            place = start // room
            last = place * room + counts[place] - 1
            code = [lists[jnp.minimum(start + i, last)] for i in range(BATCH)]
            work.append((place, [(c // slots, c % slots) for c in code]))
        scores = []
        for place, code in work:
            query = jnp.concatenate([query_ref[source, slot] for source, slot in code], axis=0)
            scores.append(
                lax.dot_general(
                    query, kv_ref[place, :length], NT, preferred_element_type=jnp.float32
                )
            )
        parts = [softmax_parts(score, scale) for score in scores]
        for (place, code), (weight, total, top) in zip(work, parts):
            mixed = jnp.dot(
                weight.astype(jnp.bfloat16),
                kv_ref[place, length : 2 * length],
                preferred_element_type=jnp.float32,
            )
            mixed = (mixed / total).astype(jnp.bfloat16)
            hi = top.astype(jnp.bfloat16).astype(jnp.float32)
            rest = top - hi
            mid = rest.astype(jnp.bfloat16).astype(jnp.float32)
            rest = (rest - mid) + jnp.log(total)
            low = rest.astype(jnp.bfloat16).astype(jnp.float32)
            last = rest - low
            for i, (source, slot) in enumerate(code):
                part = slice(i * QROWS, (i + 1) * QROWS)
                out_ref[source, slot] = mixed[part]
                value = jnp.where(
                    piece < 2,
                    jnp.where(piece == 0, hi[part], mid[part]),
                    jnp.where(piece == 2, low[part], last[part]),
                )
                stat[source] = jnp.where(within == slot, value, stat[source])
        return carry

    lax.fori_loop(0, (count + 1) // 2, one_pair, 0)
    out_ref[:, slots] = stat[...].astype(jnp.bfloat16)


def visit(note, query, kv):
    sources, tiles = query.shape[:2]
    held = kv.shape[0]
    room = 2 * CORES * SIDE
    return pl.pallas_call(
        visit_kernel,
        out_shape=jax.ShapeDtypeStruct((sources, tiles + 1) + query.shape[2:], query.dtype),
        in_specs=[pl.BlockSpec(memory_space=pltpu.VMEM)] * 2
        + [pl.BlockSpec(memory_space=pl.ANY)],
        out_specs=pl.BlockSpec(memory_space=pltpu.VMEM),
        scratch_shapes=[
            pltpu.VMEM(kv.shape, kv.dtype),
            pltpu.VMEM((sources, QROWS, HD), jnp.float32),
            pltpu.VMEM((sources, HD), jnp.int32),
            pltpu.SMEM((sources, HD), jnp.int32),
            pltpu.SMEM((held * room,), jnp.int32),
            pltpu.SMEM((held,), jnp.int32),
            pltpu.SMEM((held * room // BATCH,), jnp.int32),
            pltpu.SemaphoreType.DMA((2,)),
        ],
        compiler_params=pltpu.CompilerParams(vmem_limit_bytes=24 << 20),
        name="visit",
    )(note, query, kv)


def suffix_kernel(length_ref, query_ref, key_ref, value_ref, out_ref, top_ref, total_ref):
    kv_heads, rows = query_ref.shape[:2]
    span = key_ref.shape[1]
    cache = span - 16
    scale = 1.0 / HD**0.5
    base = pl.program_id(0) * rows
    slot = lax.broadcasted_iota(jnp.int32, (QROWS, span), 1)
    step = lax.broadcasted_iota(jnp.int32, (QROWS, span), 0) // GROUP
    fresh = (slot >= cache) & (slot - cache <= step)
    cols = [slice(k * HD, (k + 1) * HD) for k in range(kv_heads)]
    items = [(k, r) for r in range(rows) for k in range(kv_heads)]
    scores = []
    for k, r in items:
        score = lax.dot_general(
            query_ref[k, r], key_ref[r, :, cols[k]], NT, preferred_element_type=jnp.float32
        )
        live = fresh | (slot < jnp.minimum(length_ref[base + r], cache))
        scores.append(jnp.where(live, score, -jnp.inf))
    weight, total, top = softmax_parts(jnp.concatenate(scores, axis=0), scale)
    weight = weight.astype(jnp.bfloat16)
    mixed = [
        jnp.dot(
            weight[i * QROWS : (i + 1) * QROWS],
            value_ref[r, :, cols[k]],
            preferred_element_type=jnp.float32,
        )
        for i, (k, r) in enumerate(items)
    ]
    top = jnp.broadcast_to(top, (len(items) * QROWS, HD))
    total = jnp.broadcast_to(total, (len(items) * QROWS, HD))
    for i, (k, r) in enumerate(items):
        part = slice(i * QROWS, (i + 1) * QROWS)
        out_ref[k, r] = mixed[i]
        top_ref[k, r] = top[part]
        total_ref[k, r] = total[part]


def suffix(lengths, query, keys, values):
    kv_heads, rows = query.shape[:2]
    chunk = 8
    span = keys.shape[1]
    by_row = pl.BlockSpec((kv_heads, chunk, QROWS, HD), lambda i, n: (0, i, 0, 0))
    by_slot = pl.BlockSpec((chunk, span, kv_heads * HD), lambda i, n: (i, 0, 0))
    return pl.pallas_call(
        suffix_kernel,
        out_shape=(jax.ShapeDtypeStruct((kv_heads, rows, QROWS, HD), jnp.float32),) * 3,
        grid_spec=pltpu.PrefetchScalarGridSpec(
            num_scalar_prefetch=1,
            grid=(rows // chunk,),
            in_specs=[by_row, by_slot, by_slot],
            out_specs=(by_row,) * 3,
        ),
        compiler_params=pltpu.CompilerParams(vmem_limit_bytes=16 << 20),
        cost_estimate=pl.CostEstimate(
            flops=4 * rows * kv_heads * QROWS * span * HD,
            bytes_accessed=8 << 20,
            transcendentals=rows * kv_heads * QROWS * span,
        ),
        name="suffix",
    )(lengths, query, keys, values)


def join_kernel(
    core_ref, table_ref, mine_ref, theirs_ref, suf_ref, top_ref, total_ref, out_ref
):
    rows = suf_ref.shape[1]
    for which, block in enumerate((mine_ref, theirs_ref)):
        head = which ^ core_ref[0]

        def one_row(r, carry, block=block, which=which, head=head):
            far = block[table_ref[(3 * which + 1) * rows + r]].astype(jnp.float32)
            far = far + pltpu.roll(far, HD - 32, 1)
            lane = table_ref[(3 * which + 2) * rows + r]
            max_p = jnp.take_along_axis(far, jnp.full(far.shape, lane, jnp.int32), axis=1)
            log_p = jnp.take_along_axis(far, jnp.full(far.shape, lane + 64, jnp.int32), axis=1)
            max_s = top_ref[head, r]
            top = jnp.maximum(max_p, max_s)
            share_p = jnp.exp((max_p - top) + log_p)
            scale_s = jnp.exp(max_s - top)
            value = block[table_ref[3 * which * rows + r]].astype(jnp.float32)
            mixed = share_p * value + scale_s * suf_ref[head, r]
            whole = share_p + scale_s * total_ref[head, r]
            out_ref[head, r] = (mixed / whole).astype(jnp.bfloat16)
            return carry

        lax.fori_loop(0, rows, one_row, 0, unroll=8)


def join(core, table, mine, theirs, near):
    kv_heads, rows = near[0].shape[:2]
    return pl.pallas_call(
        join_kernel,
        out_shape=jax.ShapeDtypeStruct((kv_heads, rows, QROWS, HD), jnp.bfloat16),
        in_specs=[pl.BlockSpec(memory_space=pltpu.SMEM)] * 2
        + [pl.BlockSpec(memory_space=pltpu.VMEM)] * 5,
        out_specs=pl.BlockSpec(memory_space=pltpu.VMEM),
        compiler_params=pltpu.CompilerParams(vmem_limit_bytes=24 << 20),
        name="join",
    )(core, table, mine, theirs, *near)


def shards(queries, new_kv, suffix_kv, prefix_kv, prefix_id, suffix_len, owner_map):
    rows, _, width = queries.shape
    kv_heads = new_kv.shape[-1] // HD
    me = lax.axis_index("req")
    core = me % CORES

    def swap(array):
        return lax.ppermute(array, "req", SWAP)

    stored = prefix_kv[0].reshape(-1, kv_heads, HD)
    mine, other = stored[:, 0], stored[:, 1]
    mine, other = jnp.where(core == 0, mine, other), jnp.where(core == 0, other, mine)
    mine, other, prefix_id = lax.optimization_barrier((mine, other, prefix_id))
    other = swap(other)

    heads = lax.axis_size("head")
    chip_size = heads * CORES
    chips = [[c * chip_size + i for i in range(chip_size)] for c in range(SIDE * SIDE)]
    meta = jnp.stack([prefix_id[:, 0], suffix_len])
    position = core * heads + lax.axis_index("head")
    spot = jnp.arange(chip_size, dtype=jnp.int32)[:, None, None] == position
    meta = lax.psum(jnp.where(spot, meta, 0), ("req", "head"), axis_index_groups=chips)
    meta, mine, other = lax.optimization_barrier((meta, mine, other))
    kv = lax.all_gather(
        jnp.stack([mine, other]), "req", axis_index_groups=PREFIX_GROUPS, axis=0, tiled=True
    )
    ids = meta[:, 0].reshape(CORES, rows)
    lengths = lax.dynamic_index_in_dim(meta[:, 1].reshape(CORES, rows), core, 0, keepdims=False)
    ids = jnp.where(core == 0, ids, ids[::-1])
    table = owner_map.shape[0]
    picked = ids[..., None] == jnp.arange(table, dtype=jnp.int32)
    slot = jnp.sum(jnp.where(picked, owner_map, 0), axis=-1)

    def coordinate(slot, along_y):
        return jnp.where(along_y, slot // (CORES * SIDE), (slot // CORES) % SIDE)

    row = jnp.arange(rows, dtype=jnp.int32)
    before = row[None, :] < row[:, None]

    def rank_of(goal):
        same = goal[..., None, :] == goal[..., :, None]
        return jnp.sum(jnp.where(same & before, 1, 0), axis=-1)

    capacity = rows // 4
    rounds = 2
    slots = CORES * capacity
    wide, narrow = slots + 2, capacity + 1
    goal, cross_goal = coordinate(slot, core == 0), coordinate(slot, core != 0)
    rank, cross_rank = rank_of(goal), rank_of(cross_goal)
    fullest = 1 + jnp.maximum(jnp.max(rank), jnp.max(cross_rank))
    place = cross_goal * CORES + jnp.where(slot % CORES == core, 0, 1)

    query = queries.reshape(rows, STEPS, kv_heads, GROUP, HD)
    query = jnp.transpose(query, (2, 0, 1, 3, 4)).reshape(kv_heads, rows, QROWS, HD)
    own_rows = lax.dynamic_index_in_dim(query, core, 0, keepdims=False)
    other_rows = swap(lax.dynamic_index_in_dim(query, 1 - core, 0, keepdims=False))
    both = jnp.concatenate([own_rows, other_rows])

    def pack(turn):
        chip = jnp.arange(SIDE, dtype=jnp.int32)[:, None, None, None]
        spot = turn * capacity + jnp.arange(capacity, dtype=jnp.int32)[:, None]
        sent = (goal[:, None, :] == chip) & (rank[:, None, :] == spot)
        index = jnp.arange(CORES * rows, dtype=jnp.int32).reshape(CORES, 1, rows)
        from_row = jnp.sum(jnp.where(sent, index, 0), axis=-1).reshape(-1)
        places = EMPTY + jnp.sum(jnp.where(sent, place[:, None, :] - EMPTY, 0), axis=-1)
        places = places.astype(jnp.float32).reshape(SIDE, 1, slots)
        places = jnp.pad(places, ((0, 0), (0, 0), (0, HD - slots)), constant_values=EMPTY)
        at_end = jnp.arange(HD, dtype=jnp.int32) == HD - 1
        places = jnp.where(at_end, fullest.astype(jnp.float32), places)
        return send(from_row, places, both)

    def trade(blocks):
        return lax.all_to_all(blocks, "req", 0, 0, axis_index_groups=ROW_GROUPS, tiled=True)

    outgoing = pack(0)
    outgoing, lengths = lax.optimization_barrier((outgoing, lengths))
    arrived = trade(outgoing)
    pad = jnp.zeros((rows, 16 - STEPS, kv_heads * HD), jnp.bfloat16)
    keys = jnp.concatenate([suffix_kv[:, 0], new_kv[:, :, 0], pad], axis=1)
    values = jnp.concatenate([suffix_kv[:, 1], new_kv[:, :, 1], pad], axis=1)
    near = suffix(lengths, query, keys, values)
    arrived, near = lax.optimization_barrier((arrived, near))
    note = jnp.max(arrived[:, slots, 0, HD - 1].astype(jnp.float32))
    note = jnp.broadcast_to(note, (8, HD))
    note = jnp.maximum(note, swap(note))

    def come_home(done):
        back = trade(done)
        theirs = swap(back[:, capacity : slots + 1])
        fullest = jnp.max(back[:, slots + 1, 0].astype(jnp.float32))
        return back.reshape(-1, QROWS, HD), theirs.reshape(-1, QROWS, HD), fullest

    cross_goal, cross_rank = cross_goal[0], cross_rank[0]
    turn, cross_turn = rank[0] // capacity, cross_rank // capacity
    at, cross_at = rank[0] % capacity, cross_rank % capacity
    base = (turn * SIDE + goal[0]) * wide
    cross_base = (cross_turn * SIDE + cross_goal) * narrow
    home = jnp.stack(
        [
            base + at,
            base + slots,
            at,
            cross_base + cross_at,
            cross_base + capacity,
            capacity + cross_at,
        ]
    ).reshape(-1)
    which = core.reshape(1).astype(jnp.int32)
    arrived, home = lax.optimization_barrier((arrived, home))
    back, theirs, fullest = come_home(visit(note, arrived, kv))

    def finish(back, theirs, both, note, kv, near):
        return join(which, home, back, theirs, near)

    def finish_rest(back, theirs, both, note, kv, near):
        backs, others = [back], [theirs]
        for turn in range(1, rounds):
            done = visit(note, trade(pack(turn)), kv)
            more = come_home(done)
            backs.append(more[0])
            others.append(more[1])
        return join(which, home, jnp.concatenate(backs), jnp.concatenate(others), near)

    out = lax.cond(fullest <= capacity, finish, finish_rest, back, theirs, both, note, kv, near)
    out = out.reshape(kv_heads, rows, STEPS, GROUP, HD)
    return jnp.transpose(out, (1, 2, 0, 3, 4)).reshape(rows, STEPS, width)


def solution(mesh):
    return jax.shard_map(
        shards,
        mesh=mesh,
        in_specs=(
            P("req", None, "head"),
            P("req", None, None, "head"),
            P("req", None, None, "head"),
            P("req", None, None, "head"),
            P(("req", "head"), None),
            P(("req", "head")),
            P(),
        ),
        out_specs=P("req", None, "head"),
        check_vma=False,
    )
```
